128 devices in a mesh: wide: 8 (over z, core), narrow: 16 (over y, x).
Axes of the slice: x: 4, y: 4, z: 4, core: 2. Of those that a mesh axis runs over, the one named last changes fastest.
Arguments:
- amplitudes: float32 [1024, 39936], P('wide', 'narrow'), may hold values from -6 to 6
- amp_tiles: int32 [16, 624], P('wide', 'narrow'), may hold values 0 or 1
- integrals: float32 [39936, 13312], P('narrow', 'wide'), may hold values from -0.03125 to 0.03125
- int_tiles: int32 [624, 208], P('narrow', 'wide'), may hold values 0 or 1
- cycle_weight: float32 [64, 4, 8], replicated, may hold values from -1 to 1
Outputs:
- cycle_term: float32 [64, 256, 1664], P(None, 'wide', 'narrow')
The draws below stay inside these ranges and needn't reach their ends.
All inputs are finite; a program needn't handle non-finite values. No bound on the sum of `amp_tiles` or of `int_tiles` on one device may be relied on, other than what follows from the above.
Results may differ from the reference program's by a relative error of at most 0.000084.
Values sent between devices are 32-bit elements; how exact they have to be, the bound alone decides.
A program may use at most 192 MiB of HBM per device.

```python
import jax
import jax.numpy as jnp
from jax import lax

NV = 1664
NO = 256
TILE = 64
OI = 4
AW = 8
KC = 64
PAIRS = 1024
CD = 39936
AB = 13312


def with_ends(array, rng, least, top_value):
    longest = array.shape.index(max(array.shape))
    spots = []
    for shift in (0, 1):
        where = [jax.random.randint(jax.random.fold_in(rng, axis), (), 0, length) for axis, length in enumerate(array.shape)]
        where[longest] = (where[longest] + shift) % array.shape[longest]
        spots.append(tuple(where))
    return array.at[spots[0]].set(least).at[spots[1]].set(top_value)


def shard_levels(key, shape, shards, least, high):
    loudness, own = 1.0, jax.random.fold_in(key, 6)
    for axis_at, shards_of in shards:
        heights = jnp.exp(jax.random.uniform(jax.random.fold_in(own, axis_at), (shards_of,), jnp.float32, least / len(shards), high / len(shards)))
        loudness = loudness * jnp.repeat(heights, shape[axis_at] // shards_of).reshape([-1 if axis == axis_at else 1 for axis in range(len(shape))])
    return loudness


def scatter_about(own_key, extent, spread, reach, split=(), kind=jnp.bfloat16):
    array = spread * jax.random.normal(own_key, extent, jnp.float32)
    if split:
        array = array * shard_levels(own_key, extent, split, -0.22, 0.18)
    return jnp.clip(array, -reach, reach).astype(kind)


def setup_inputs(seed: int = 0) -> dict:
    key_list = jax.random.split(jax.random.key(seed), 6)
    return {
        "amplitudes": scatter_about(key_list[0], (PAIRS, CD), 1.0, 6.0, ((0, 8), (1, 16)), jnp.float32),
        "amp_tiles": with_ends((jax.random.randint(key_list[1], (PAIRS // TILE, CD // TILE), 0, 4) < 3).astype(jnp.int32), jax.random.fold_in(key_list[1], 1), 0, 1),
        "integrals": scatter_about(key_list[2], (CD, AB), CD ** -0.5, 0.03125, ((0, 16), (1, 8)), jnp.float32),
        "int_tiles": with_ends((jax.random.randint(key_list[3], (CD // TILE, AB // TILE), 0, 2) < 1).astype(jnp.int32), jax.random.fold_in(key_list[3], 1), 0, 1),
        "cycle_weight": scatter_about(key_list[4], (KC, OI, AW), (OI * AW) ** -0.5, 1.0, (), jnp.float32),
    }


def expand(block, tiles):
    rows_t, cols_t = tiles.shape
    shaped = block.reshape(rows_t, TILE, cols_t, TILE) * tiles.astype(block.dtype)[:, None, :, None]
    return shaped.reshape(block.shape)


def reference(amplitudes, amp_tiles, integrals, int_tiles, cycle_weight):
    ladder = jnp.dot(expand(amplitudes, amp_tiles), expand(integrals, int_tiles), precision=lax.Precision.HIGHEST, preferred_element_type=jnp.float32)
    ladder = ladder.reshape(OI, NO, AW, NV)
    return jnp.einsum("kia,ijab->kjb", cycle_weight, ladder, precision=lax.Precision.HIGHEST)
```

```python
import functools

import jax
import jax.numpy as jnp
from jax import lax
from jax.experimental import pallas as pl
from jax.experimental.pallas import tpu as pltpu
from jax.sharding import PartitionSpec as P

MESH = pl.DeviceIdType.MESH
F32 = jnp.float32
BF16 = jnp.bfloat16
TILE = 64
K = 2496
KP = 2560
KB = 256
NK = KP // KB
M = 1664
PIECE = 104
CUT = 56
CHUNK = 4 * PIECE
OFF = (2, 1, 3, 0)
NT = (((1,), (1,)), ((), ()))


def dot_nt(a, b):
    return lax.dot_general(a, b, NT, preferred_element_type=F32)


def split(value):
    high = value.astype(BF16)
    return high, (value - high.astype(F32)).astype(BF16)


def spread(flags, columns):
    tiles = flags.shape[1]
    row = lax.broadcasted_iota(jnp.int32, (tiles, columns), 0)
    lane = lax.broadcasted_iota(jnp.int32, (tiles, columns), 1)
    pick = jnp.where(lane // TILE == row, 1.0, 0.0).astype(BF16)
    return jnp.dot(flags.astype(F32).astype(BF16), pick, preferred_element_type=F32)


def kernel(
    amp, amp_tiles, ints, int_tiles, weight, out,
    amp_in, int_in, amps, flags, int_hi, int_lo, amp_hi, amp_lo, part,
    r1, r2, r3, r4, turned, regrouped, w_hi, w_lo,
    load_sem, z_send, z_recv, c_send, c_recv, s_send, s_recv, a_send, a_recv,
):
    wide, narrow = lax.axis_index("wide"), lax.axis_index("narrow")
    z, core = wide // 2, wide % 2
    y, x = narrow // 4, narrow % 4

    def at_z(step):
        return (((z + step) % 4) * 2 + core, narrow)

    def at_x(step):
        return (wide, y * 4 + (x + step) % 4)

    def at_y(step):
        return (wide, ((y + step) % 4) * 4 + x)

    sibling = (z * 2 + 1 - core, narrow)

    load_amp = pltpu.make_async_copy(amp, amp_in, load_sem.at[2])
    load_amp.start()

    def load_int(step, slot):
        return pltpu.make_async_copy(ints.at[pl.ds(step * KB, KB)], int_in.at[slot], load_sem.at[slot])

    rest = K - (NK - 1) * KB
    load_last = pltpu.make_async_copy(
        ints.at[pl.ds((NK - 1) * KB, rest)], int_in.at[(NK - 1) % 2, pl.ds(0, rest)], load_sem.at[(NK - 1) % 2]
    )
    load_int(0, 0).start()
    load_int(1, 1).start()

    barrier = pltpu.get_barrier_semaphore()
    for step in range(1, 8):
        pl.semaphore_signal(barrier, inc=1, device_id=((wide + step) % 8, narrow), device_id_type=MESH)
    for device in (at_x(1), at_x(3), at_y(1), at_y(3)):
        pl.semaphore_signal(barrier, inc=1, device_id=device, device_id_type=MESH)

    amp_flags = spread(amp_tiles[...], K)
    load_amp.wait()
    half_rows = [pl.ds(pl.multiple_of(h * 128 + core * 64, 64), 64) for h in range(2)]
    for h in range(2):
        amps[0, half_rows[h], pl.ds(0, K)] = amp_in[pl.ds(h * 64, 64), :] * amp_flags[h : h + 1, :]
        amps[0, half_rows[h], pl.ds(K, KP - K)] = jnp.zeros((64, KP - K), F32)
    pl.semaphore_wait(barrier, 11)

    sent = []

    def send(src, dst, send_sem, recv_sem, device):
        copy = pltpu.make_async_remote_copy(
            src_ref=src, dst_ref=dst, send_sem=send_sem, recv_sem=recv_sem, device_id=device, device_id_type=MESH
        )
        return copy

    def z_copy(index):
        step, kind = (1, index) if index < 3 else (3, index - 3)
        side = 0 if index < 3 else 1
        if kind < 2:
            src = amps.at[0, half_rows[(kind + side) % 2]]
        else:
            src = amps.at[1, half_rows[side]]
        return send(src, amps.at[kind + 1, half_rows[side]], z_send.at[index], z_recv.at[index], at_z(step))

    def c_copy(block, side):
        ref = amps.at[block, half_rows[side]]
        return send(ref, ref, c_send.at[block, side], c_recv.at[block, side], sibling)

    zs = [z_copy(i) for i in range(6)]
    cs = [[c_copy(b, s) for s in range(2)] for b in range(4)]
    for i in (0, 3):
        zs[i].start()
    for s in range(2):
        cs[0][s].start()
    for i in (1, 4):
        zs[i].start()

    int_flags = spread(int_tiles[...], M)
    for step in range(NK):
        count = min(4, K // TILE - step * 4)
        flags[step, pl.ds(0, count), :] = int_flags[step * 4 : step * 4 + count, :]

    def prepare(step, slot, rows):
        for half in range(2):
            for col in range(M // 128):
                cols = pl.ds(col * 128, 128)
                parts = []
                for t in range(2):
                    first = half * 128 + t * 64
                    if first < rows:
                        flag = flags[step, pl.ds(half * 2 + t, 1), cols]
                        parts.append(int_in[slot, pl.ds(first, 64), cols] * flag)
                    else:
                        parts.append(jnp.zeros((64, 128), F32))
                high, low = split(jnp.concatenate(parts, axis=0).T)
                int_hi[step, cols, pl.ds(half * 128, 128)] = high
                int_lo[step, cols, pl.ds(half * 128, 128)] = low

    def prepare_step(step, _):
        slot = step % 2
        load_int(step, slot).wait()
        prepare(step, slot, KB)

        @pl.when(step + 2 < NK - 1)
        def _():
            load_int(step + 2, slot).start()

        @pl.when(step + 2 == NK - 1)
        def _():
            load_last.start()

        return 0

    lax.fori_loop(0, NK - 1, prepare_step, 0)
    load_last.wait()
    prepare(NK - 1, (NK - 1) % 2, rest)

    def spread_weight(piece):
        r = lax.broadcasted_iota(jnp.int32, (512, 64), 0)
        c = lax.broadcasted_iota(jnp.int32, (512, 64), 1)
        rows = jnp.where(r // 8 == c, 1.0, 0.0).astype(BF16)
        r2_ = lax.broadcasted_iota(jnp.int32, (8, 64), 0)
        c2_ = lax.broadcasted_iota(jnp.int32, (8, 64), 1)
        cols = jnp.where(c2_ // 8 == r2_, 1.0, 0.0).astype(BF16)
        wide_piece = jnp.dot(piece, cols, preferred_element_type=F32).astype(BF16)
        tall = jnp.dot(rows, wide_piece, preferred_element_type=F32)
        return jnp.where(r % 8 == c % 8, tall, 0.0).astype(BF16)

    for i in range(4):
        high, low = split(weight[:, i, :])
        w_hi[:, pl.ds(i * 64, 64)] = spread_weight(high)
        w_lo[:, pl.ds(i * 64, 64)] = spread_weight(low)

    along = ((at_x, at_y), (at_y, at_x))

    def place(half, ra, rb):
        first, second = (x, y) if half == 0 else (y, x)
        pa, pb = (first + ra) % 4, (second + rb) % 4
        py, px = (pb, pa) if half == 0 else (pa, pb)
        return pl.ds(pl.multiple_of(py * CHUNK + px * PIECE, 8), PIECE)

    def off(r):
        if isinstance(r, int):
            return OFF[r]
        return jnp.where(r == 0, 2, jnp.where(r == 1, 1, jnp.where(r == 2, 3, 0)))

    def cols_of(half):
        return pl.ds(half * 128, 128)

    def s1p1(q, half, rb):
        step = (1 if rb < 2 else 3) if isinstance(rb, int) else jnp.where(rb < 2, 1, 3)
        src = part.at[q, place(half, 2, off(rb)), cols_of(half)]
        return send(src, r1.at[q, half, rb], s_send.at[q, half, rb], s_recv.at[q, half, rb], along[half][0](step))

    def s1p2(q, half, side, rb):
        step = (1 + 2 * side) if isinstance(side, int) else jnp.where(side == 0, 1, 3)
        src = part.at[q, place(half, step, off(rb)), cols_of(half)]
        index = 4 + side * 4 + rb
        return send(
            src, r2.at[q, half, side, rb], s_send.at[q, half, index], s_recv.at[q, half, index], along[half][0](step)
        )

    def s2_rows(side):
        return (0, CUT) if side == 0 else (CUT, PIECE - CUT)

    def s2p1(q, half, side):
        start, size = s2_rows(side)
        whole = place(half, 0, 2)
        rows = pl.ds(pl.multiple_of(whole.start + start, 8), size)
        index = 12 + side
        return send(
            part.at[q, rows, cols_of(half)], r3.at[q, half, side, pl.ds(0, size)],
            s_send.at[q, half, index], s_recv.at[q, half, index], along[half][1](1 + 2 * side),
        )

    def s2p2(q, half, side):
        step = 1 + 2 * side
        index = 14 + side
        return send(
            part.at[q, place(half, 0, step), cols_of(half)], r4.at[q, half, side],
            s_send.at[q, half, index], s_recv.at[q, half, index], along[half][1](step),
        )

    def after_chunk(q, ry):
        near = jnp.where(ry < 2, 1, 0)
        s1p1(q, 0, ry).start()
        s1p2(q, 0, near, ry).start()

        @pl.when(ry == 0)
        def _():
            for rb in range(4):
                s1p1(q, 1, rb).start()

        for side in range(2):

            @pl.when(ry == 1 + side)
            def _():
                for rb in (2, 3) if side == 0 else (0, 1):
                    s1p2(q, 1, side, rb).start()

    def first_sums(q):
        for half in range(2):
            for rb in range(4):
                side = 0 if rb < 2 else 1
                s1p1(q, half, rb).wait_recv()
                rows = place(half, 1 + 2 * side, off(rb))
                part[q, rows, cols_of(half)] += r1[q, half, rb]
                s1p2(q, half, side, rb).start()

    def own_sums(q):
        for rb in range(4):
            for half in range(2):
                for side in range(2):
                    s1p2(q, half, side, rb).wait_recv()
                part[q, place(half, 0, off(rb)), cols_of(half)] += r2[q, half, 0, rb] + r2[q, half, 1, rb]
                if rb == 0:
                    for side in range(2):
                        s2p1(q, half, side).start()

    def second_sums(q):
        for half in range(2):
            for side in range(2):
                s2p1(q, half, side).wait_recv()
                start, size = s2_rows(side)
                whole = place(half, 0, 1 + 2 * side)
                rows = pl.ds(pl.multiple_of(whole.start + start, 8), size)
                part[q, rows, cols_of(half)] += r3[q, half, side, pl.ds(0, size)]
                s2p2(q, half, side).start()

    def group(q, dest):
        dc, dh, dl = dest // 4, (dest // 2) % 2, dest % 2
        if q == 0:
            return dh * 4 + dc * 2 + dl, z
        if q == 1:
            return dh * 4 + dc * 2 + dl, (z + 3 + 2 * dh) % 4
        if q == 2:
            return (1 - dh) * 4 + dc * 2 + dl, (z + 1 + 2 * dh) % 4
        return dh * 4 + dc * 2 + dl, (z + 2) % 4

    def regroup(q, step):
        dest = (wide + step) % 8
        position, i = group(q, dest)
        src = turned.at[q, pl.ds(pl.multiple_of(position * 32, 32), 32)]
        return send(src, regrouped.at[i, wide], a_send.at[q, step], a_recv.at[q, step], (dest, narrow))

    def last_sums(q):
        for half in range(2):
            for side in range(2):
                s2p2(q, half, side).wait_recv()
            total = part[q, place(half, 0, 0), cols_of(half)] + r4[q, half, 0] + r4[q, half, 1]
            total = jnp.concatenate([total, jnp.zeros((128 - PIECE, 128), F32)], axis=0)
            turned[q, cols_of(half), :] = total.T
        for step in range(1, 8):
            regroup(q, step).start()
        position, i = group(q, wide)
        regrouped[i, wide] = turned[q, pl.ds(pl.multiple_of(position * 32, 32), 32), :]

    def multiply(q):
        for k in range(NK):
            high, low = split(amps[q, :, pl.ds(k * KB, KB)])
            amp_hi[k] = high
            amp_lo[k] = low

        def chunk(ry, _):
            rows = pl.ds(pl.multiple_of(((y + off(ry)) % 4) * CHUNK, 8), CHUNK)
            total = None
            for k in range(NK):
                term = dot_nt(int_hi[k, rows], amp_hi[k]) + dot_nt(int_hi[k, rows], amp_lo[k])
                term = term + dot_nt(int_lo[k, rows], amp_hi[k])
                total = term if total is None else total + term
            part[q, rows, :] = total
            after_chunk(q, ry)
            if q > 0:

                @pl.when(ry == 0)
                def _():
                    second_sums(q - 1)

                @pl.when(ry == 2)
                def _():
                    last_sums(q - 1)

            return 0

        lax.fori_loop(0, 4, chunk, 0)

    for q in range(4):
        if q > 0:
            for side in range(2):
                zs[3 * side + q - 1].wait_recv()
                cs[q][side].start()
                if q == 1:
                    zs[3 * side + 2].start()
        for side in range(2):
            cs[q][side].wait_recv()
        multiply(q)
        first_sums(q)
        own_sums(q)
    second_sums(3)
    last_sums(3)

    for q in range(4):
        for step in range(1, 8):
            regroup(q, step).wait_recv()
    for g in range(4):
        value = regrouped[:, :, pl.ds(g * 8, 8), :].reshape(256, 128)
        high, low = split(value)
        total = jnp.dot(w_hi[...], high, preferred_element_type=F32)
        total += jnp.dot(w_hi[...], low, preferred_element_type=F32)
        total += jnp.dot(w_lo[...], high, preferred_element_type=F32)
        out[:, pl.ds(g * 8, 8), :] = total.reshape(64, 8, 128)[:, :, :PIECE]

    for copy in zs:
        copy.wait_send()
    for block in cs:
        for copy in block:
            copy.wait_send()
    for q in range(4):
        for half in range(2):
            for rb in range(4):
                s1p1(q, half, rb).wait_send()
                for side in range(2):
                    s1p2(q, half, side, rb).wait_send()
            for side in range(2):
                s2p1(q, half, side).wait_send()
                s2p2(q, half, side).wait_send()
        for step in range(1, 8):
            regroup(q, step).wait_send()


def shards(amplitudes, amp_tiles, integrals, int_tiles, cycle_weight):
    vmem = pl.BlockSpec(memory_space=pltpu.VMEM)
    hbm = pl.BlockSpec(memory_space=pl.ANY)
    dma = pltpu.SemaphoreType.DMA
    return pl.pallas_call(
        kernel,
        out_shape=jax.ShapeDtypeStruct((64, 32, PIECE), F32),
        in_specs=[hbm, vmem, hbm, vmem, vmem],
        out_specs=vmem,
        scratch_shapes=[
            pltpu.VMEM((128, K), F32),
            pltpu.VMEM((2, KB, M), F32),
            pltpu.VMEM((4, 256, KP), F32),
            pltpu.VMEM((NK, 8, M), F32),
            pltpu.VMEM((NK, M, KB), BF16),
            pltpu.VMEM((NK, M, KB), BF16),
            pltpu.VMEM((NK, 256, KB), BF16),
            pltpu.VMEM((NK, 256, KB), BF16),
            pltpu.VMEM((4, M, 256), F32),
            pltpu.VMEM((4, 2, 4, PIECE, 128), F32),
            pltpu.VMEM((4, 2, 2, 4, PIECE, 128), F32),
            pltpu.VMEM((4, 2, 2, CUT, 128), F32),
            pltpu.VMEM((4, 2, 2, PIECE, 128), F32),
            pltpu.VMEM((4, 256, 128), F32),
            pltpu.VMEM((4, 8, 32, 128), F32),
            pltpu.VMEM((512, 256), BF16),
            pltpu.VMEM((512, 256), BF16),
            dma((3,)),
            dma((6,)),
            dma((6,)),
            dma((4, 2)),
            dma((4, 2)),
            dma((4, 2, 16)),
            dma((4, 2, 16)),
            dma((4, 8)),
            dma((4, 8)),
        ],
        compiler_params=pltpu.CompilerParams(
            collective_id=0, has_side_effects=True, vmem_limit_bytes=60 * 1024 * 1024
        ),
        cost_estimate=pl.CostEstimate(
            flops=6 * 1024 * KP * M, bytes_accessed=4 * (K * M + 128 * K + 64 * 32 * 128), transcendentals=0
        ),
    )(amplitudes, amp_tiles, integrals, int_tiles, cycle_weight)


def solution(mesh):
    placed = (
        P("wide", "narrow"),
        P("wide", "narrow"),
        P("narrow", "wide"),
        P("narrow", "wide"),
        P(),
    )
    return jax.shard_map(
        shards, mesh=mesh, in_specs=placed, out_specs=P(None, "wide", "narrow"), check_vma=False
    )
```

```python
import functools

import jax
import jax.numpy as jnp
from jax import lax
from jax.experimental import pallas as pl
from jax.experimental.pallas import tpu as pltpu
from jax.sharding import PartitionSpec as P

MESH = pl.DeviceIdType.MESH
F32 = jnp.float32
BF16 = jnp.bfloat16
TILE = 64
K = 2496
KP = 2560
KB = 256
NK = KP // KB
M = 1664
PIECE = 104
CHUNK = 4 * PIECE
CUT = 56
LAST = 3
SPLIT = 6
CUTS = (pl.ds(0, SPLIT * KB), pl.ds(SPLIT * KB, KP - SPLIT * KB))
OFF = (2, 1, 3, 0)
NT = (((1,), (1,)), ((), ()))


def dot_nt(a, b):
    return lax.dot_general(a, b, NT, preferred_element_type=F32)


def split(value):
    high = value.astype(BF16)
    return high, (value - high.astype(F32)).astype(BF16)


def pick(tiles, columns):
    row = lax.broadcasted_iota(jnp.int32, (tiles, columns), 0)
    lane = lax.broadcasted_iota(jnp.int32, (tiles, columns), 1)
    return jnp.where(lane // TILE == row, 1.0, 0.0).astype(BF16)


def kernel(
    amp, amp_tiles, ints, int_tiles, weight, out,
    amp_in, int_in, amps, flags, int_hi, int_lo, amp_hi, amp_lo, part,
    r1, r2, r3, r4, r5, r6, turned, regrouped, w_hi, w_lo,
    load_sem, z_send, z_recv, c_send, c_recv, s_send, s_recv, a_send, a_recv,
):
    wide, narrow = lax.axis_index("wide"), lax.axis_index("narrow")
    z, core = wide // 2, wide % 2
    y, x = narrow // 4, narrow % 4

    def at_z(step):
        return (((z + step) % 4) * 2 + core, narrow)

    def at_x(step):
        return (wide, y * 4 + (x + step) % 4)

    def at_y(step):
        return (wide, ((y + step) % 4) * 4 + x)

    sibling = (z * 2 + 1 - core, narrow)

    load_amp = pltpu.make_async_copy(amp, amp_in, load_sem.at[2])
    load_amp.start()

    def load_int(step, slot):
        return pltpu.make_async_copy(ints.at[pl.ds(step * KB, KB)], int_in.at[slot], load_sem.at[slot])

    rest = K - (NK - 1) * KB
    load_last = pltpu.make_async_copy(
        ints.at[pl.ds((NK - 1) * KB, rest)], int_in.at[(NK - 1) % 2, pl.ds(0, rest)], load_sem.at[(NK - 1) % 2]
    )
    load_int(0, 0).start()
    load_int(1, 1).start()

    barrier = pltpu.get_barrier_semaphore()
    for step in range(1, 8):
        pl.semaphore_signal(barrier, inc=1, device_id=((wide + step) % 8, narrow), device_id_type=MESH)
    for device in (at_x(1), at_x(3), at_y(1), at_y(3)):
        pl.semaphore_signal(barrier, inc=1, device_id=device, device_id_type=MESH)

    amp_flags = amp_tiles[...].astype(F32).astype(BF16)
    amp_flags = jnp.dot(amp_flags, pick(K // TILE, KP), preferred_element_type=F32)
    load_amp.wait()
    half_rows = [pl.ds(pl.multiple_of(h * 128 + core * 64, 64), 64) for h in range(2)]
    for step in range(KP // 128):
        first = step * 128
        value = amp_in[pl.ds(first, min(128, K - first)), :]
        if first + 128 > K:
            value = jnp.concatenate([value, jnp.zeros((first + 128 - K, 128), F32)], axis=0)
        value = value.T
        for h in range(2):
            flag = amp_flags[h : h + 1, first : first + 128]
            amps[0, half_rows[h], pl.ds(first, 128)] = value[h * 64 : h * 64 + 64, :] * flag
    pl.semaphore_wait(barrier, 11)

    def send(src, dst, send_sem, recv_sem, device):
        copy = pltpu.make_async_remote_copy(
            src_ref=src, dst_ref=dst, send_sem=send_sem, recv_sem=recv_sem, device_id=device, device_id_type=MESH
        )
        return copy

    def z_copy(side, kind, cut):
        src, dst = (0, (kind + side) % 2) if kind < 2 else (1, side), (kind + 1, side)
        index = (side * 3 + kind) * 2 + cut
        return send(
            amps.at[src[0], half_rows[src[1]], CUTS[cut]], amps.at[dst[0], half_rows[dst[1]], CUTS[cut]],
            z_send.at[index], z_recv.at[index], at_z(1 + 2 * side),
        )

    def c_copy(block, side, cut):
        ref = amps.at[block, half_rows[side], CUTS[cut]]
        index = (block * 2 + side) * 2 + cut
        return send(ref, ref, c_send.at[index], c_recv.at[index], sibling)

    def start_z(kind):
        for cut in range(2):
            for side in range(2):
                z_copy(side, kind, cut).start()

    def swap(block, cut):
        for side in range(2):
            z_copy(side, block - 1, cut).wait_recv()
            c_copy(block, side, cut).start()

    def have(block, cut):
        for side in range(2):
            c_copy(block, side, cut).wait_recv()

    start_z(0)
    for cut in range(2):
        for side in range(2):
            c_copy(0, side, cut).start()
    start_z(1)

    int_flags = int_tiles[...].astype(F32).astype(BF16)
    int_flags = lax.dot_general(int_flags, pick(M // TILE, M), (((0,), (0,)), ((), ())), preferred_element_type=F32)
    for step in range(NK):
        count = min(4, K // TILE - step * 4)
        flags[step, pl.ds(0, count), :] = int_flags[step * 4 : step * 4 + count, :]

    def prepare(step, slot, rows):
        for half in range(2):
            for col in range(M // 128):
                cols = pl.ds(col * 128, 128)
                parts = []
                for t in range(2):
                    first = half * 128 + t * 64
                    if first < rows:
                        flag = flags[step, pl.ds(half * 2 + t, 1), cols]
                        parts.append(int_in[slot, pl.ds(first, 64), cols] * flag)
                    else:
                        parts.append(jnp.zeros((64, 128), F32))
                high, low = split(jnp.concatenate(parts, axis=0).T)
                int_hi[step, cols, pl.ds(half * 128, 128)] = high
                int_lo[step, cols, pl.ds(half * 128, 128)] = low

    def prepare_step(step, _):
        slot = step % 2
        load_int(step, slot).wait()
        prepare(step, slot, KB)

        @pl.when(step + 2 < NK - 1)
        def _():
            load_int(step + 2, slot).start()

        @pl.when(step + 2 == NK - 1)
        def _():
            load_last.start()

        return 0

    lax.fori_loop(0, NK - 1, prepare_step, 0)
    load_last.wait()
    prepare(NK - 1, (NK - 1) % 2, rest)

    def spread_weight(piece):
        r = lax.broadcasted_iota(jnp.int32, (512, 64), 0)
        c = lax.broadcasted_iota(jnp.int32, (512, 64), 1)
        rows = jnp.where(r // 8 == c, 1.0, 0.0).astype(BF16)
        from_a = lax.broadcasted_iota(jnp.int32, (8, 64), 0)
        to_a = lax.broadcasted_iota(jnp.int32, (8, 64), 1) // 8
        columns = jnp.where(from_a == to_a, 1.0, 0.0).astype(BF16)
        tall = dot_nt(rows, piece).astype(BF16)
        return jnp.where(r % 8 == c % 8, jnp.dot(tall, columns, preferred_element_type=F32), 0.0).astype(BF16)

    for i in range(4):
        high, low = split(weight[i])
        w_hi[:, pl.ds(i * 64, 64)] = spread_weight(high)
        w_lo[:, pl.ds(i * 64, 64)] = spread_weight(low)

    along = ((at_x, at_y), (at_y, at_x))

    def place(half, ra, rb):
        first, second = (x, y) if half == 0 else (y, x)
        pa, pb = (first + ra) % 4, (second + rb) % 4
        py, px = (pb, pa) if half == 0 else (pa, pb)
        return pl.ds(pl.multiple_of(py * CHUNK + px * PIECE, 8), PIECE)

    def off(r):
        if isinstance(r, int):
            return OFF[r]
        return jnp.where(r == 0, 2, jnp.where(r == 1, 1, jnp.where(r == 2, 3, 0)))

    def cols_of(half):
        return pl.ds(half * 128, 128)

    def rows_of(ry):
        return pl.ds(pl.multiple_of(((y + off(ry)) % 4) * CHUNK, 8), CHUNK)

    def first_copy(q, ra, rb):
        src = part.at[q, place(0, off(ra), off(rb)), cols_of(0)]
        index = ra * 4 + rb
        return send(
            src, r1.at[0, ra, pl.ds(rb * PIECE, PIECE)], s_send.at[q, 0, index], s_recv.at[q, 0, index],
            at_x(off(ra)),
        )

    def first_copy_rows(q, ra):
        return send(
            part.at[q, rows_of(ra), cols_of(1)], r1.at[1, ra], s_send.at[q, 1, ra], s_recv.at[q, 1, ra],
            at_y(off(ra)),
        )

    def second_copy(q, half, rb):
        src = part.at[q, place(half, 0, off(rb)), cols_of(half)]
        index = 12 + rb
        return send(
            src, r2.at[half, rb], s_send.at[q, half, index], s_recv.at[q, half, index], along[half][1](off(rb))
        )

    def s1p1(q, half, rb):
        step = (1 if rb < 2 else 3) if isinstance(rb, int) else jnp.where(rb < 2, 1, 3)
        src = part.at[q, place(half, 2, off(rb)), cols_of(half)]
        return send(src, r3.at[q, half, rb], s_send.at[q, half, rb], s_recv.at[q, half, rb], along[half][0](step))

    def s1p2(q, half, side, rb):
        step = (1 + 2 * side) if isinstance(side, int) else jnp.where(side == 0, 1, 3)
        src = part.at[q, place(half, step, off(rb)), cols_of(half)]
        index = 4 + side * 4 + rb
        return send(
            src, r4.at[q, half, side, rb], s_send.at[q, half, index], s_recv.at[q, half, index], along[half][0](step)
        )

    def s2_rows(side):
        return (0, CUT) if side == 0 else (CUT, PIECE - CUT)

    def s2p1(q, half, side):
        start, size = s2_rows(side)
        whole = place(half, 0, 2)
        rows = pl.ds(pl.multiple_of(whole.start + start, 8), size)
        index = 12 + side
        return send(
            part.at[q, rows, cols_of(half)], r5.at[q, half, side, pl.ds(0, size)],
            s_send.at[q, half, index], s_recv.at[q, half, index], along[half][1](1 + 2 * side),
        )

    def s2p2(q, half, side):
        step = 1 + 2 * side
        index = 14 + side
        return send(
            part.at[q, place(half, 0, step), cols_of(half)], r6.at[q, half, side],
            s_send.at[q, half, index], s_recv.at[q, half, index], along[half][1](step),
        )

    def ring_after_chunk(q, ry):
        near = jnp.where(ry < 2, 1, 0)
        s1p1(q, 0, ry).start()
        s1p2(q, 0, near, ry).start()

        @pl.when(ry == 0)
        def _():
            for rb in range(4):
                s1p1(q, 1, rb).start()

        for side in range(2):

            @pl.when(ry == 1 + side)
            def _():
                for rb in (2, 3) if side == 0 else (0, 1):
                    s1p2(q, 1, side, rb).start()

    def pass_on(q, half, rb):
        side = 0 if rb < 2 else 1
        s1p1(q, half, rb).wait_recv()
        rows = place(half, 1 + 2 * side, off(rb))
        part[q, rows, cols_of(half)] += r3[q, half, rb]
        s1p2(q, half, side, rb).start()

    def ring_own_sum(q, half, rb):
        for side in range(2):
            s1p2(q, half, side, rb).wait_recv()
        part[q, place(half, 0, off(rb)), cols_of(half)] += r4[q, half, 0, rb] + r4[q, half, 1, rb]
        if rb == 0:
            for side in range(2):
                s2p1(q, half, side).start()

    def pass_on_second(q, half, side):
        s2p1(q, half, side).wait_recv()
        start, size = s2_rows(side)
        whole = place(half, 0, 1 + 2 * side)
        rows = pl.ds(pl.multiple_of(whole.start + start, 8), size)
        part[q, rows, cols_of(half)] += r5[q, half, side, pl.ds(0, size)]
        s2p2(q, half, side).start()

    def after_chunk(q, ry):
        if q < LAST:
            ring_after_chunk(q, ry)
            return

        @pl.when(ry < 3)
        def _():
            first_copy_rows(q, ry).start()

        for ra in range(3):
            first_copy(q, ra, ry).start()

    def ring_own_sums(q):
        for rb in range(4):
            for half in (1, 0):
                ring_own_sum(q, half, rb)

    def pass_all(q):
        for rb in range(4):
            for half in (1, 0):
                pass_on(q, half, rb)

    def second_sums(q):
        for half in (1, 0):
            for side in range(2):
                pass_on_second(q, half, side)

    def own_sums(q):
        for ra in range(3):
            first_copy_rows(q, ra).wait_recv()
        for rb in range(4):
            for half in (1, 0):
                if half == 0:
                    for ra in range(3):
                        first_copy(q, ra, rb).wait_recv()
                    here = [pl.ds(rb * PIECE, PIECE)] * 3
                else:
                    here = [pl.ds(pl.multiple_of(((x + off(rb)) % 4) * PIECE, 8), PIECE)] * 3
                total = part[q, place(half, 0, off(rb)), cols_of(half)]
                for ra in range(3):
                    total = total + r1[half, ra, here[ra]]
                part[q, place(half, 0, off(rb)), cols_of(half)] = total
                if rb < 3:
                    second_copy(q, half, rb).start()

    def group(q, dest):
        dc, dh, dl = dest // 4, (dest // 2) % 2, dest % 2
        if q == 0:
            return dh * 4 + dc * 2 + dl, z
        if q == 1:
            return dh * 4 + dc * 2 + dl, (z + 3 + 2 * dh) % 4
        if q == 2:
            return (1 - dh) * 4 + dc * 2 + dl, (z + 1 + 2 * dh) % 4
        return dh * 4 + dc * 2 + dl, (z + 2) % 4

    def regroup(q, step):
        dest = (wide + step) % 8
        position, i = group(q, dest)
        src = turned.at[q, pl.ds(pl.multiple_of(position * 32, 32), 32)]
        return send(src, regrouped.at[i, wide], a_send.at[q, step], a_recv.at[q, step], (dest, narrow))

    def last_sum(q, half):
        total = part[q, place(half, 0, 0), cols_of(half)]
        if q < LAST:
            for side in range(2):
                s2p2(q, half, side).wait_recv()
            total = total + r6[q, half, 0] + r6[q, half, 1]
        else:
            for rb in range(3):
                second_copy(q, half, rb).wait_recv()
                total = total + r2[half, rb]
        total = jnp.concatenate([total, jnp.zeros((128 - PIECE, 128), F32)], axis=0)
        turned[q, cols_of(half), :] = total.T

    def hand_out(q):
        for step in range(1, 8):
            regroup(q, step).start()
        position, i = group(q, wide)
        regrouped[i, wide] = turned[q, pl.ds(pl.multiple_of(position * 32, 32), 32), :]

    def last_sums(q):
        for half in (1, 0):
            last_sum(q, half)
        hand_out(q)

    def split_block(q, steps):
        for k in steps:
            high, low = split(amps[q, :, pl.ds(k * KB, KB)])
            amp_hi[k] = high
            amp_lo[k] = low

    def product(rows, steps):
        total = None
        for k in steps:
            term = dot_nt(int_hi[k, rows], amp_hi[k]) + dot_nt(int_hi[k, rows], amp_lo[k])
            term = term + dot_nt(int_lo[k, rows], amp_hi[k])
            total = term if total is None else total + term
        return total

    def multiply_first(q, steps, slots):
        split_block(q, steps)

        def chunk(ry, _):
            rows = rows_of(ry)
            part[q, rows, :] = product(rows, steps)
            for at, action in slots:
                pl.when(ry == at)(action)
            return 0

        lax.fori_loop(0, 4, chunk, 0)

    def multiply(q, steps, slots):
        split_block(q, steps)

        def chunk(ry, _):
            rows = rows_of(ry)
            total = product(rows, steps)
            part[q, rows, :] = total if len(steps) == NK else part[q, rows, :] + total
            after_chunk(q, ry)

            for at, action in slots:
                pl.when(ry == at)(action)
            return 0

        lax.fori_loop(0, 4, chunk, 0)

    every = range(NK)
    front, back = every[:SPLIT], every[SPLIT:]
    have(0, 0)
    have(0, 1)
    multiply(0, every, ((2, lambda: swap(1, 0)),))
    have(1, 0)
    multiply_first(1, front, ((1, lambda: swap(1, 1)), (3, lambda: pass_all(0))))
    start_z(2)
    have(1, 1)
    multiply(1, back, ())
    ring_own_sums(0)
    swap(2, 0)
    have(2, 0)
    multiply_first(2, front, (
        (0, lambda: pass_all(1)), (1, lambda: second_sums(0)), (2, lambda: swap(2, 1)),
    ))
    have(2, 1)
    multiply(2, back, ((0, lambda: ring_own_sums(1)), (2, lambda: last_sums(0))))
    second_sums(1)
    swap(3, 0)
    pass_all(2)
    have(3, 0)
    multiply_first(3, front, ((1, lambda: last_sums(1)),))
    swap(3, 1)
    ring_own_sums(2)
    have(3, 1)
    multiply(3, back, ((3, lambda: second_sums(2)),))
    own_sums(3)
    last_sums(2)
    last_sums(3)

    for q in range(4):
        for step in range(1, 8):
            regroup(q, step).wait_recv()
    for g in range(4):
        value = regrouped[:, :, pl.ds(g * 8, 8), :].reshape(256, 128)
        high, low = split(value)
        total = jnp.dot(w_hi[...], high, preferred_element_type=F32)
        total += jnp.dot(w_hi[...], low, preferred_element_type=F32)
        total += jnp.dot(w_lo[...], high, preferred_element_type=F32)
        out[:, pl.ds(g * 8, 8), :] = total.reshape(64, 8, 128)[:, :, :PIECE]

    for side in range(2):
        for cut in range(2):
            for kind in range(3):
                z_copy(side, kind, cut).wait_send()
            for block in range(4):
                c_copy(block, side, cut).wait_send()
    for q in range(4):
        if q < LAST:
            for half in range(2):
                for rb in range(4):
                    s1p1(q, half, rb).wait_send()
                    for side in range(2):
                        s1p2(q, half, side, rb).wait_send()
                for side in range(2):
                    s2p1(q, half, side).wait_send()
                    s2p2(q, half, side).wait_send()
        else:
            for half in range(2):
                for rb in range(3):
                    second_copy(q, half, rb).wait_send()
            for ra in range(3):
                first_copy_rows(q, ra).wait_send()
                for rb in range(4):
                    first_copy(q, ra, rb).wait_send()
        for step in range(1, 8):
            regroup(q, step).wait_send()


def shards(amplitudes, amp_tiles, integrals, int_tiles, cycle_weight):
    vmem = pl.BlockSpec(memory_space=pltpu.VMEM)
    hbm = pl.BlockSpec(memory_space=pl.ANY)
    dma = pltpu.SemaphoreType.DMA
    return pl.pallas_call(
        kernel,
        out_shape=jax.ShapeDtypeStruct((64, 32, PIECE), F32),
        in_specs=[hbm, vmem, hbm, vmem, vmem],
        out_specs=vmem,
        scratch_shapes=[
            pltpu.VMEM((K, 128), F32),
            pltpu.VMEM((2, KB, M), F32),
            pltpu.VMEM((4, 256, KP), F32),
            pltpu.VMEM((NK, 8, M), F32),
            pltpu.VMEM((NK, M, KB), BF16),
            pltpu.VMEM((NK, M, KB), BF16),
            pltpu.VMEM((NK, 256, KB), BF16),
            pltpu.VMEM((NK, 256, KB), BF16),
            pltpu.VMEM((4, M, 256), F32),
            pltpu.VMEM((2, 3, CHUNK, 128), F32),
            pltpu.VMEM((2, 3, PIECE, 128), F32),
            pltpu.VMEM((LAST, 2, 4, PIECE, 128), F32),
            pltpu.VMEM((LAST, 2, 2, 4, PIECE, 128), F32),
            pltpu.VMEM((LAST, 2, 2, CUT, 128), F32),
            pltpu.VMEM((LAST, 2, 2, PIECE, 128), F32),
            pltpu.VMEM((4, 256, 128), F32),
            pltpu.VMEM((4, 8, 32, 128), F32),
            pltpu.VMEM((512, 256), BF16),
            pltpu.VMEM((512, 256), BF16),
            dma((3,)),
            dma((12,)),
            dma((12,)),
            dma((16,)),
            dma((16,)),
            dma((4, 2, 16)),
            dma((4, 2, 16)),
            dma((4, 8)),
            dma((4, 8)),
        ],
        compiler_params=pltpu.CompilerParams(
            collective_id=0, has_side_effects=True, vmem_limit_bytes=60 * 1024 * 1024
        ),
        cost_estimate=pl.CostEstimate(
            flops=6 * 1024 * KP * M, bytes_accessed=4 * (K * M + 128 * K + 64 * 32 * 128), transcendentals=0
        ),
    )(amplitudes.T, amp_tiles, integrals, int_tiles.T, cycle_weight.transpose(1, 2, 0))


def solution(mesh):
    placed = (
        P("wide", "narrow"),
        P("wide", "narrow"),
        P("narrow", "wide"),
        P("narrow", "wide"),
        P(),
    )
    return jax.shard_map(
        shards, mesh=mesh, in_specs=placed, out_specs=P(None, "wide", "narrow"), check_vma=False
    )
```

```python
import functools

import jax
import jax.numpy as jnp
from jax import lax
from jax.experimental import pallas as pl
from jax.experimental.pallas import tpu as pltpu
from jax.sharding import PartitionSpec as P

MESH = pl.DeviceIdType.MESH
F32 = jnp.float32
BF16 = jnp.bfloat16
TILE = 64
K = 2496
KP = 2560
KB = 256
NK = KP // KB
M = 1664
PIECE = 104
CHUNK = 4 * PIECE
LAST = 3
SPLIT = 6
CUTS = (pl.ds(0, SPLIT * KB), pl.ds(SPLIT * KB, KP - SPLIT * KB))
OFF = (2, 1, 3, 0)
NT = (((1,), (1,)), ((), ()))


def dot_nt(a, b):
    return lax.dot_general(a, b, NT, preferred_element_type=F32)


def split(value):
    high = value.astype(BF16)
    return high, (value - high.astype(F32)).astype(BF16)


def pick(tiles, columns):
    row = lax.broadcasted_iota(jnp.int32, (tiles, columns), 0)
    lane = lax.broadcasted_iota(jnp.int32, (tiles, columns), 1)
    return jnp.where(lane // TILE == row, 1.0, 0.0).astype(BF16)


def kernel(
    amp, amp_tiles, ints, int_tiles, weight, out,
    amp_in, int_in, amps, flags, int_hi, int_lo, amp_hi, amp_lo, part,
    r1, r2, r3, r4, turned, regrouped, w_hi, w_lo,
    load_sem, z_send, z_recv, c_send, c_recv, s_send, s_recv, a_send, a_recv,
):
    wide, narrow = lax.axis_index("wide"), lax.axis_index("narrow")
    z, core = wide // 2, wide % 2
    y, x = narrow // 4, narrow % 4

    def at_z(step):
        return (((z + step) % 4) * 2 + core, narrow)

    def at_x(step):
        return (wide, y * 4 + (x + step) % 4)

    def at_y(step):
        return (wide, ((y + step) % 4) * 4 + x)

    sibling = (z * 2 + 1 - core, narrow)

    load_amp = pltpu.make_async_copy(amp, amp_in, load_sem.at[2])
    load_amp.start()

    def load_int(step, slot):
        return pltpu.make_async_copy(ints.at[pl.ds(step * KB, KB)], int_in.at[slot], load_sem.at[slot])

    rest = K - (NK - 1) * KB
    load_last = pltpu.make_async_copy(
        ints.at[pl.ds((NK - 1) * KB, rest)], int_in.at[(NK - 1) % 2, pl.ds(0, rest)], load_sem.at[(NK - 1) % 2]
    )
    load_int(0, 0).start()
    load_int(1, 1).start()

    barrier = pltpu.get_barrier_semaphore()
    for step in range(1, 8):
        pl.semaphore_signal(barrier, inc=1, device_id=((wide + step) % 8, narrow), device_id_type=MESH)
    for device in (at_x(1), at_x(3), at_y(1), at_y(3)):
        pl.semaphore_signal(barrier, inc=1, device_id=device, device_id_type=MESH)

    amp_flags = amp_tiles[...].astype(F32).astype(BF16)
    amp_flags = jnp.dot(amp_flags, pick(K // TILE, KP), preferred_element_type=F32)
    load_amp.wait()
    half_rows = [pl.ds(pl.multiple_of(h * 128 + core * 64, 64), 64) for h in range(2)]
    def mask(steps):
        for step in steps:
            first = step * 128
            value = amp_in[pl.ds(first, min(128, K - first)), :]
            if first + 128 > K:
                value = jnp.concatenate([value, jnp.zeros((first + 128 - K, 128), F32)], axis=0)
            value = value.T
            for h in range(2):
                flag = amp_flags[h : h + 1, first : first + 128]
                amps[0, half_rows[h], pl.ds(first, 128)] = value[h * 64 : h * 64 + 64, :] * flag

    def send(src, dst, send_sem, recv_sem, device):
        copy = pltpu.make_async_remote_copy(
            src_ref=src, dst_ref=dst, send_sem=send_sem, recv_sem=recv_sem, device_id=device, device_id_type=MESH
        )
        return copy

    def z_copy(side, kind, cut):
        src, dst = (0, (kind + side) % 2) if kind < 2 else (1, side), (kind + 1, side)
        index = (side * 3 + kind) * 2 + cut
        return send(
            amps.at[src[0], half_rows[src[1]], CUTS[cut]], amps.at[dst[0], half_rows[dst[1]], CUTS[cut]],
            z_send.at[index], z_recv.at[index], at_z(1 + 2 * side),
        )

    def c_copy(block, side, cut):
        ref = amps.at[block, half_rows[side], CUTS[cut]]
        index = (block * 2 + side) * 2 + cut
        return send(ref, ref, c_send.at[index], c_recv.at[index], sibling)

    def start_z(kind):
        for cut in range(2):
            for side in range(2):
                z_copy(side, kind, cut).start()

    def swap(block, cut):
        for side in range(2):
            z_copy(side, block - 1, cut).wait_recv()
            c_copy(block, side, cut).start()

    def have(block, cut):
        for side in range(2):
            c_copy(block, side, cut).wait_recv()

    mask(range(KP // 128))
    pl.semaphore_wait(barrier, 11)
    for cut in range(2):
        for side in range(2):
            z_copy(side, 0, cut).start()
        for side in range(2):
            c_copy(0, side, cut).start()
    start_z(1)

    int_flags = int_tiles[...].astype(F32).astype(BF16)
    int_flags = lax.dot_general(int_flags, pick(M // TILE, M), (((0,), (0,)), ((), ())), preferred_element_type=F32)
    for step in range(NK):
        count = min(4, K // TILE - step * 4)
        flags[step, pl.ds(0, count), :] = int_flags[step * 4 : step * 4 + count, :]

    def prepare(step, slot, rows):
        for half in range(2):
            for col in range(M // 128):
                cols = pl.ds(col * 128, 128)
                parts = []
                for t in range(2):
                    first = half * 128 + t * 64
                    if first < rows:
                        flag = flags[step, pl.ds(half * 2 + t, 1), cols]
                        parts.append(int_in[slot, pl.ds(first, 64), cols] * flag)
                    else:
                        parts.append(jnp.zeros((64, 128), F32))
                high, low = split(jnp.concatenate(parts, axis=0).T)
                int_hi[step, cols, pl.ds(half * 128, 128)] = high
                int_lo[step, cols, pl.ds(half * 128, 128)] = low

    def prepare_step(step, _):
        slot = step % 2
        load_int(step, slot).wait()
        prepare(step, slot, KB)

        @pl.when(step + 2 < NK - 1)
        def _():
            load_int(step + 2, slot).start()

        @pl.when(step + 2 == NK - 1)
        def _():
            load_last.start()

        return 0

    lax.fori_loop(0, NK - 1, prepare_step, 0)
    load_last.wait()
    prepare(NK - 1, (NK - 1) % 2, rest)

    def spread_weight(piece):
        r = lax.broadcasted_iota(jnp.int32, (512, 64), 0)
        c = lax.broadcasted_iota(jnp.int32, (512, 64), 1)
        rows = jnp.where(r // 8 == c, 1.0, 0.0).astype(BF16)
        from_a = lax.broadcasted_iota(jnp.int32, (8, 64), 0)
        to_a = lax.broadcasted_iota(jnp.int32, (8, 64), 1) // 8
        columns = jnp.where(from_a == to_a, 1.0, 0.0).astype(BF16)
        tall = dot_nt(rows, piece).astype(BF16)
        return jnp.where(r % 8 == c % 8, jnp.dot(tall, columns, preferred_element_type=F32), 0.0).astype(BF16)

    for i in range(4):
        high, low = split(weight[i])
        w_hi[:, pl.ds(i * 64, 64)] = spread_weight(high)
        w_lo[:, pl.ds(i * 64, 64)] = spread_weight(low)

    along = ((at_x, at_y), (at_y, at_x))

    def place(half, ra, rb):
        first, second = (x, y) if half == 0 else (y, x)
        pa, pb = (first + ra) % 4, (second + rb) % 4
        py, px = (pb, pa) if half == 0 else (pa, pb)
        return pl.ds(pl.multiple_of(py * CHUNK + px * PIECE, 8), PIECE)

    def off(r):
        if isinstance(r, int):
            return OFF[r]
        return jnp.where(r == 0, 2, jnp.where(r == 1, 1, jnp.where(r == 2, 3, 0)))

    def cols_of(half):
        return pl.ds(half * 128, 128)

    def rows_of(ry):
        return pl.ds(pl.multiple_of(((y + off(ry)) % 4) * CHUNK, 8), CHUNK)

    def first_copy(q, ra, rb):
        src = part.at[q, place(0, off(ra), off(rb)), cols_of(0)]
        index = ra * 4 + rb
        return send(
            src, r1.at[0, ra, pl.ds(rb * PIECE, PIECE)], s_send.at[q, 0, index], s_recv.at[q, 0, index],
            at_x(off(ra)),
        )

    def first_copy_rows(q, ra):
        return send(
            part.at[q, rows_of(ra), cols_of(1)], r1.at[1, ra], s_send.at[q, 1, ra], s_recv.at[q, 1, ra],
            at_y(off(ra)),
        )

    def second_copy(q, half, rb):
        src = part.at[q, place(half, 0, off(rb)), cols_of(half)]
        index = 12 + rb
        return send(
            src, r2.at[q, half, rb], s_send.at[q, half, index], s_recv.at[q, half, index], along[half][1](off(rb))
        )

    def s1p1(q, half, rb):
        step = (1 if rb < 2 else 3) if isinstance(rb, int) else jnp.where(rb < 2, 1, 3)
        src = part.at[q, place(half, 2, off(rb)), cols_of(half)]
        return send(src, r3.at[q, half, rb], s_send.at[q, half, rb], s_recv.at[q, half, rb], along[half][0](step))

    def s1p2(q, half, side, rb):
        step = (1 + 2 * side) if isinstance(side, int) else jnp.where(side == 0, 1, 3)
        src = part.at[q, place(half, step, off(rb)), cols_of(half)]
        index = 4 + side * 4 + rb
        return send(
            src, r4.at[q, half, side, rb], s_send.at[q, half, index], s_recv.at[q, half, index], along[half][0](step)
        )

    def ring_after_chunk(q, ry):
        near = jnp.where(ry < 2, 1, 0)
        s1p1(q, 0, ry).start()
        s1p2(q, 0, near, ry).start()

        @pl.when(ry == 0)
        def _():
            for rb in range(4):
                s1p1(q, 1, rb).start()

        for side in range(2):

            @pl.when(ry == 1 + side)
            def _():
                for rb in (2, 3) if side == 0 else (0, 1):
                    s1p2(q, 1, side, rb).start()

    def pass_on(q, half, rb):
        side = 0 if rb < 2 else 1
        s1p1(q, half, rb).wait_recv()
        rows = place(half, 1 + 2 * side, off(rb))
        part[q, rows, cols_of(half)] += r3[q, half, rb]
        s1p2(q, half, side, rb).start()

    def ring_own_sum(q, half, rb):
        for side in range(2):
            s1p2(q, half, side, rb).wait_recv()
        part[q, place(half, 0, off(rb)), cols_of(half)] += r4[q, half, 0, rb] + r4[q, half, 1, rb]
        if rb < 3:
            second_copy(q, half, rb).start()

    def after_chunk(q, ry):
        if q < LAST:
            ring_after_chunk(q, ry)
            return

        @pl.when(ry < 3)
        def _():
            first_copy_rows(q, ry).start()

        for ra in range(3):
            first_copy(q, ra, ry).start()

    def ring_own_sums(q):
        for rb in range(4):
            for half in (1, 0):
                ring_own_sum(q, half, rb)

    def pass_all(q):
        for rb in range(4):
            for half in (1, 0):
                pass_on(q, half, rb)

    def own_sums(q):
        for ra in range(3):
            first_copy_rows(q, ra).wait_recv()
        for rb in range(4):
            for half in (1, 0):
                if half == 0:
                    for ra in range(3):
                        first_copy(q, ra, rb).wait_recv()
                    here = [pl.ds(rb * PIECE, PIECE)] * 3
                else:
                    here = [pl.ds(pl.multiple_of(((x + off(rb)) % 4) * PIECE, 8), PIECE)] * 3
                total = part[q, place(half, 0, off(rb)), cols_of(half)]
                for ra in range(3):
                    total = total + r1[half, ra, here[ra]]
                part[q, place(half, 0, off(rb)), cols_of(half)] = total
                if rb < 3:
                    second_copy(q, half, rb).start()

    def group(q, dest):
        dc, dh, dl = dest // 4, (dest // 2) % 2, dest % 2
        if q == 0:
            return dh * 4 + dc * 2 + dl, z
        if q == 1:
            return dh * 4 + dc * 2 + dl, (z + 3 + 2 * dh) % 4
        if q == 2:
            return (1 - dh) * 4 + dc * 2 + dl, (z + 1 + 2 * dh) % 4
        return dh * 4 + dc * 2 + dl, (z + 2) % 4

    def regroup(q, step):
        dest = (wide + step) % 8
        position, i = group(q, dest)
        src = turned.at[q, pl.ds(pl.multiple_of(position * 32, 32), 32)]
        return send(src, regrouped.at[i, wide], a_send.at[q, step], a_recv.at[q, step], (dest, narrow))

    def last_sum(q, half):
        total = part[q, place(half, 0, 0), cols_of(half)]
        for rb in range(3):
            second_copy(q, half, rb).wait_recv()
            total = total + r2[q, half, rb]
        total = jnp.concatenate([total, jnp.zeros((128 - PIECE, 128), F32)], axis=0)
        turned[q, cols_of(half), :] = total.T

    def hand_out(q):
        for step in (4, 3, 5, 2, 6, 1, 7):
            regroup(q, step).start()
        position, i = group(q, wide)
        regrouped[i, wide] = turned[q, pl.ds(pl.multiple_of(position * 32, 32), 32), :]

    def last_sums(q):
        for half in (1, 0):
            last_sum(q, half)
        hand_out(q)

    def split_block(q, steps):
        for k in steps:
            high, low = split(amps[q, :, pl.ds(k * KB, KB)])
            amp_hi[k] = high
            amp_lo[k] = low

    def product(rows, steps):
        total = None
        for k in steps:
            term = dot_nt(int_hi[k, rows], amp_hi[k]) + dot_nt(int_hi[k, rows], amp_lo[k])
            term = term + dot_nt(int_lo[k, rows], amp_hi[k])
            total = term if total is None else total + term
        return total

    def multiply_first(q, steps, slots):
        split_block(q, steps)

        def chunk(ry, _):
            rows = rows_of(ry)
            part[q, rows, :] = product(rows, steps)
            for at, action in slots:
                pl.when(ry == at)(action)
            return 0

        lax.fori_loop(0, 4, chunk, 0)

    def multiply(q, steps, slots):
        split_block(q, steps)

        def chunk(ry, _):
            rows = rows_of(ry)
            total = product(rows, steps)
            part[q, rows, :] = total if len(steps) == NK else part[q, rows, :] + total
            after_chunk(q, ry)

            for at, action in slots:
                pl.when(ry == at)(action)
            return 0

        lax.fori_loop(0, 4, chunk, 0)

    every = range(NK)
    front, back = every[:SPLIT], every[SPLIT:]
    have(0, 0)
    have(0, 1)
    multiply(0, every, ((2, lambda: swap(1, 0)),))
    have(1, 0)
    multiply_first(1, front, ((1, lambda: swap(1, 1)), (3, lambda: pass_all(0))))
    start_z(2)
    have(1, 1)
    multiply(1, back, ())
    swap(2, 0)
    have(2, 0)
    multiply_first(2, front, ((0, lambda: ring_own_sums(0)), (1, lambda: pass_all(1)), (2, lambda: swap(2, 1))))
    have(2, 1)
    multiply(2, back, ((1, lambda: last_sums(0)),))
    ring_own_sums(1)
    swap(3, 0)
    have(3, 0)
    multiply_first(3, front, ((0, lambda: pass_all(2)), (2, lambda: last_sums(1)),))
    swap(3, 1)
    ring_own_sums(2)
    have(3, 1)
    multiply(3, back, ((3, lambda: last_sums(2)),))
    own_sums(3)
    last_sums(3)

    for q in range(4):
        for step in range(1, 8):
            regroup(q, step).wait_recv()
    for g in range(4):
        value = regrouped[:, :, pl.ds(g * 8, 8), :].reshape(256, 128)
        high, low = split(value)
        total = jnp.dot(w_hi[...], high, preferred_element_type=F32)
        total += jnp.dot(w_hi[...], low, preferred_element_type=F32)
        total += jnp.dot(w_lo[...], high, preferred_element_type=F32)
        out[:, pl.ds(g * 8, 8), :] = total.reshape(64, 8, 128)[:, :, :PIECE]

    for side in range(2):
        for cut in range(2):
            for kind in range(3):
                z_copy(side, kind, cut).wait_send()
            for block in range(4):
                c_copy(block, side, cut).wait_send()
    for q in range(4):
        for half in range(2):
            for rb in range(3):
                second_copy(q, half, rb).wait_send()
        if q < LAST:
            for half in range(2):
                for rb in range(4):
                    s1p1(q, half, rb).wait_send()
                    for side in range(2):
                        s1p2(q, half, side, rb).wait_send()
        else:
            for ra in range(3):
                first_copy_rows(q, ra).wait_send()
                for rb in range(4):
                    first_copy(q, ra, rb).wait_send()
        for step in range(1, 8):
            regroup(q, step).wait_send()


def shards(amplitudes, amp_tiles, integrals, int_tiles, cycle_weight):
    vmem = pl.BlockSpec(memory_space=pltpu.VMEM)
    hbm = pl.BlockSpec(memory_space=pl.ANY)
    dma = pltpu.SemaphoreType.DMA
    return pl.pallas_call(
        kernel,
        out_shape=jax.ShapeDtypeStruct((64, 32, PIECE), F32),
        in_specs=[hbm, vmem, hbm, vmem, vmem],
        out_specs=vmem,
        scratch_shapes=[
            pltpu.VMEM((K, 128), F32),
            pltpu.VMEM((2, KB, M), F32),
            pltpu.VMEM((4, 256, KP), F32),
            pltpu.VMEM((NK, 8, M), F32),
            pltpu.VMEM((NK, M, KB), BF16),
            pltpu.VMEM((NK, M, KB), BF16),
            pltpu.VMEM((NK, 256, KB), BF16),
            pltpu.VMEM((NK, 256, KB), BF16),
            pltpu.VMEM((4, M, 256), F32),
            pltpu.VMEM((2, 3, CHUNK, 128), F32),
            pltpu.VMEM((4, 2, 3, PIECE, 128), F32),
            pltpu.VMEM((LAST, 2, 4, PIECE, 128), F32),
            pltpu.VMEM((LAST, 2, 2, 4, PIECE, 128), F32),
            pltpu.VMEM((4, 256, 128), F32),
            pltpu.VMEM((4, 8, 32, 128), F32),
            pltpu.VMEM((512, 256), BF16),
            pltpu.VMEM((512, 256), BF16),
            dma((3,)),
            dma((12,)),
            dma((12,)),
            dma((16,)),
            dma((16,)),
            dma((4, 2, 16)),
            dma((4, 2, 16)),
            dma((4, 8)),
            dma((4, 8)),
        ],
        compiler_params=pltpu.CompilerParams(
            collective_id=0, has_side_effects=True, vmem_limit_bytes=60 * 1024 * 1024
        ),
        cost_estimate=pl.CostEstimate(
            flops=6 * 1024 * KP * M, bytes_accessed=4 * (K * M + 128 * K + 64 * 32 * 128), transcendentals=0
        ),
    )(amplitudes.T, amp_tiles, integrals, int_tiles.T, cycle_weight.transpose(1, 2, 0))


def solution(mesh):
    placed = (
        P("wide", "narrow"),
        P("wide", "narrow"),
        P("narrow", "wide"),
        P("narrow", "wide"),
        P(),
    )
    return jax.shard_map(
        shards, mesh=mesh, in_specs=placed, out_specs=P(None, "wide", "narrow"), check_vma=False
    )
```
